32 devices in a mesh: seq: 8 (over z, x), rep: 4 (over y, core).
Axes of the slice: x: 2, y: 2, z: 4, core: 2. Of those that a mesh axis runs over, the one named last changes fastest.
Arguments:
- tokens: bfloat16 [4, 2048, 1024], P('rep', 'seq'), may hold values from -6 to 6
- cotangent: bfloat16 [4, 2048, 1024], P('rep', 'seq'), may hold values from -6 to 6
- segment_ids: int32 [4, 2048], P('rep', 'seq'), may hold values from -1 to 2, as said below
- input_gain: bfloat16 [1024], P(('seq', 'rep')), may hold values from 0.5 to 1.5
- ssm_input: bfloat16 [1024, 3072], P(('seq', 'rep')), may hold values from -0.1875 to 0.1875
- state_proj: bfloat16 [1024, 256], P(('seq', 'rep')), may hold values from -0.02734375 to 0.02734375
- step_proj: bfloat16 [1024, 24], P(('seq', 'rep')), may hold values from -0.1875 to 0.1875
- ssm_output: bfloat16 [1024, 1536], P(('seq', 'rep')), may hold values from -0.0390625 to 0.0390625
- qkv_proj: bfloat16 [1024, 768], P(('seq', 'rep')), may hold values from -0.1875 to 0.1875
- attn_output: bfloat16 [1024, 512], P(('seq', 'rep')), may hold values from -3 to 3
- ffn_gain: bfloat16 [1024], P(('seq', 'rep')), may hold values from 0.5 to 1.5
- gate_up: bfloat16 [1024, 4096], P(('seq', 'rep')), may hold values from -0.1875 to 0.1875
- down_proj: bfloat16 [1024, 2048], P(('seq', 'rep')), may hold values from -0.125 to 0.125
- head_params: float32 [3, 24], replicated, may hold values from -13 to 2, as said below
Outputs:
- layer_out: bfloat16 [4, 2048, 1024], P('rep', 'seq')
- input_grad: bfloat16 [4, 2048, 1024], P('rep', 'seq')
- input_gain_grad: float32 [1024], P(('seq', 'rep'))
- ssm_input_grad: float32 [1024, 3072], P(('seq', 'rep'))
- state_proj_grad: float32 [1024, 256], P(('seq', 'rep'))
- step_proj_grad: float32 [1024, 24], P(('seq', 'rep'))
- ssm_output_grad: float32 [1024, 1536], P(('seq', 'rep'))
- qkv_proj_grad: float32 [1024, 768], P(('seq', 'rep'))
- attn_output_grad: float32 [1024, 512], P(('seq', 'rep'))
- ffn_gain_grad: float32 [1024], P(('seq', 'rep'))
- gate_up_grad: float32 [1024, 4096], P(('seq', 'rep'))
- down_proj_grad: float32 [1024, 2048], P(('seq', 'rep'))
- head_params_grad: float32 [3, 24], replicated
The draws below stay inside these ranges and needn't reach their ends.
Inputs may be any that keep to these rules, and one draw needn't show every extreme that they name: `segment_ids`: per group, live rows carry a sequence number 0, 1 or 2 and padding rows -1. Rows form blocks of 32; a device's 8 slots hold 6 to 8 used blocks first, the rest padding; the last device of seq and one other use all 8. Each sequence fills a run of consecutive used blocks in row order and is live on a leading part of its last block. Sequence 1 has live rows on the first and on the last device of seq. `head_params`: row 0 holds logarithms of decay rates, row 1 step biases, row 2 skip weights.
All inputs are finite; a program needn't handle non-finite values.
Results may differ from the reference program's by a relative error of at most 0.014.
Values may be sent and summed in bfloat16 or wider, within the bound.
A program may use at most 256 MiB of HBM per device.

```python
import math
import jax
import jax.numpy as jnp
from jax import lax

D = 1024
FF = 2048
HEADS = 8
KV_HEADS = 2
HEAD_DIM = 64
SSM_HEADS = 24
SSM_DIM = 64
STATE = 128
BLOCK = 32
SLOTS = 8
ROWS_DEV = 256
GROUP_ROWS = 2048
GROUPS = 4
D_SSM = 1536


def group_segments(key):
    first_key, second_key, third_key = jax.random.split(key, 3)
    devices = GROUP_ROWS // ROWS_DEV
    least = max(1, 4 * SLOTS // 5)
    counts = jax.random.randint(first_key, (devices,), least, SLOTS + 1)
    full_at = jax.random.randint(second_key, (), 0, devices)
    places = jnp.arange(devices)
    counts = jnp.where((places == full_at) | (places == devices - 1), SLOTS, counts)
    tails = jax.random.randint(third_key, (3,), 1, BLOCK)
    rows = jnp.arange(GROUP_ROWS)
    device = rows // ROWS_DEV
    slot = rows % ROWS_DEV // BLOCK
    within = rows % BLOCK
    before = jnp.cumsum(counts) - counts
    used = slot < counts[device]
    number = before[device] + slot
    total = jnp.sum(counts)
    head_end = counts[0] - 1
    long_end = total - counts[devices - 1]
    sequence = jnp.where(number < head_end, 0, jnp.where(number <= long_end, 1, 2))
    last_block = jnp.where(sequence == 0, head_end - 1, jnp.where(sequence == 1, long_end, total - 1))
    live = used & ((number != last_block) | (within < tails[sequence]))
    return jnp.where(live, sequence, -1).astype(jnp.int32)


def draw_segment_ids(key, part):
    key = jax.random.fold_in(key, 11)
    keys = jax.random.split(key, GROUPS)
    return jax.vmap(group_segments)(keys)


def draw_head_params(key, part):
    key = jax.random.fold_in(key, 5)
    rate_key, bias_key, skip_key = jax.random.split(key, 3)
    rates = jnp.exp(jax.random.uniform(rate_key, (SSM_HEADS,), jnp.float32, math.log(0.2 / GROUP_ROWS), math.log(0.08)))
    bias = jax.random.uniform(bias_key, (SSM_HEADS,), jnp.float32, -1.0, 1.0)
    skip = jax.random.uniform(skip_key, (SSM_HEADS,), jnp.float32, 0.5, 1.5)
    return jnp.stack([jnp.log(rates), bias, skip]).astype(jnp.float32)


def block_scale(key, dims, shards, low, largest):
    level = 1.0
    for axis_at, shards_of in shards:
        heights = jax.random.uniform(jax.random.fold_in(jax.random.fold_in(key, 6), axis_at), (shards_of,), jnp.float32, low / len(shards), largest / len(shards))
        level = level * jnp.repeat(jnp.exp(heights), dims[axis_at] // shards_of).reshape((-1,) + (1,) * (len(dims) - 1 - axis_at))
    return level


def bell_draw(rng, extent, deviation, reach, cuts=(), kind=jnp.bfloat16):
    values = deviation * jax.random.normal(rng, extent, jnp.float32)
    if cuts:
        values = values * block_scale(rng, extent, cuts, -0.22, 0.18)
    return jnp.clip(values, -reach, reach).astype(kind)


def setup_inputs(seed: int = 0) -> dict:
    arg_keys = jax.random.split(jax.random.key(seed), 15)
    return {
        "tokens": bell_draw(arg_keys[0], (GROUPS, GROUP_ROWS, D), 1.0, 6.0, ((0, 4), (1, 8))),
        "cotangent": bell_draw(arg_keys[1], (GROUPS, GROUP_ROWS, D), 1.0, 6.0, ((0, 4), (1, 8))),
        "segment_ids": draw_segment_ids(jax.random.fold_in(arg_keys[14], 71), 0),
        "input_gain": jnp.clip(1.0 + 0.1 * jax.random.normal(arg_keys[3], (D,), jnp.float32), 0.5, 1.5).astype(jnp.bfloat16),
        "ssm_input": bell_draw(arg_keys[4], (D, 2 * D_SSM), D ** -0.5, 0.1875, ((0, 32),)),
        "state_proj": bell_draw(arg_keys[5], (D, 2 * STATE), (44 * D) ** -0.5, 0.02734375, ((0, 32),)),
        "step_proj": bell_draw(arg_keys[6], (D, SSM_HEADS), D ** -0.5, 0.1875, ((0, 32),)),
        "ssm_output": bell_draw(arg_keys[7], (D, D_SSM), (16 * D_SSM) ** -0.5, 0.0390625, ((0, 32),)),
        "qkv_proj": bell_draw(arg_keys[8], (D, HEADS * HEAD_DIM + 2 * KV_HEADS * HEAD_DIM), D ** -0.5, 0.1875, ((0, 32),)),
        "attn_output": bell_draw(arg_keys[9], (D, HEADS * HEAD_DIM), 4 ** -0.5, 3.0, ((0, 32),)),
        "ffn_gain": jnp.clip(1.0 + 0.1 * jax.random.normal(arg_keys[10], (D,), jnp.float32), 0.5, 1.5).astype(jnp.bfloat16),
        "gate_up": bell_draw(arg_keys[11], (D, 2 * FF), D ** -0.5, 0.1875, ((0, 32),)),
        "down_proj": bell_draw(arg_keys[12], (D, FF), FF ** -0.5, 0.125, ((0, 32),)),
        "head_params": draw_head_params(jax.random.fold_in(arg_keys[14], 71), 0),
    }


EPS = 1e-06
HIGH = lax.Precision.HIGHEST

@jax.custom_vjp
def low(v):
    return lax.optimization_barrier(v.astype(jnp.bfloat16)).astype(jnp.float32)

@jax.custom_vjp
def low_back(v):
    return v

def low_keep(v):
    return (low(v), None)

def low_pass(kept, grad):
    return (grad,)

def back_keep(v):
    return (v, None)

def back_low(kept, grad):
    return (low(grad),)
low.defvjp(low_keep, low_pass)
low_back.defvjp(back_keep, back_low)

def rounded(values):
    return low_back(low(values))

def matmul(left, right):
    return jnp.dot(left, right, precision=HIGH, preferred_element_type=jnp.float32)

def norm_rows(values, gain):
    return values * lax.rsqrt(lax.optimization_barrier(jnp.mean(values * values, axis=-1, keepdims=True)) + EPS) * gain

def stretch_math(state, signal, entry_map, read_map, step_size, log_decay, restarts):
    length = signal.shape[0]
    cumul = jnp.cumsum(log_decay, axis=0)
    counter = jnp.cumsum(restarts, axis=0)
    places = jnp.arange(length)
    joined = (counter[:, None] == counter[None, :]) & (places[None, :] <= places[:, None])
    spread = cumul.T[:, :, None] - cumul.T[:, None, :]
    decay = jnp.where(joined[None], jnp.exp(jnp.where(joined[None], spread, 0.0)), 0.0)
    intersection = jnp.dot(read_map, entry_map.T, precision=HIGH)
    mixing = decay * intersection[None] * step_size.T[:, None, :]
    within = jnp.einsum('hts,shp->thp', mixing, signal, precision=HIGH)
    opening = jnp.where((counter == 0)[:, None], jnp.exp(cumul), 0.0)
    carried = jnp.einsum('tn,hpn->thp', read_map, state, precision=HIGH) * opening[:, :, None]
    closing = jnp.where((counter == counter[-1])[:, None], jnp.exp(cumul[-1][None, :] - cumul), 0.0)
    scaled = signal * (closing * step_size)[:, :, None]
    renewed = opening[-1][:, None, None] * state + jnp.einsum('shp,sn->hpn', scaled, entry_map, precision=HIGH)
    return (within + carried, renewed, opening)

def mamba_group(inner, states, step_raw, head_params, segments):
    rows = inner.shape[0]
    gate = inner[:, :D_SSM].reshape(rows, SSM_HEADS, SSM_DIM)
    signal = inner[:, D_SSM:].reshape(rows, SSM_HEADS, SSM_DIM)
    step_size = jax.nn.softplus(step_raw + head_params[1])
    log_decay = -step_size * jnp.exp(head_params[0])
    earlier = jnp.concatenate([jnp.full((1,), -7, jnp.int32), segments[:-1]])
    restarts = jnp.where(segments != earlier, jnp.ones_like(step_raw[:, 0]), jnp.zeros_like(step_raw[:, 0]))
    count = rows // BLOCK
    pieces = (signal.reshape(count, BLOCK, SSM_HEADS, SSM_DIM), states[:, :STATE].reshape(count, BLOCK, STATE), states[:, STATE:].reshape(count, BLOCK, STATE), step_size.reshape(count, BLOCK, SSM_HEADS), log_decay.reshape(count, BLOCK, SSM_HEADS), restarts.reshape(count, BLOCK))

    def advance(state, piece):
        part, renewed, opening = stretch_math(state, *piece)
        return (renewed, part)
    start = jnp.zeros((SSM_HEADS, SSM_DIM, STATE), inner.dtype)
    final, parts = lax.scan(jax.checkpoint(advance), start, pieces)
    mixed = parts.reshape(rows, SSM_HEADS, SSM_DIM) + head_params[2][None, :, None] * signal
    return (mixed * jax.nn.silu(gate)).reshape(rows, D_SSM)

def attend_group(projected, segments):
    rows = projected.shape[0]
    width = HEADS * HEAD_DIM
    kv_width = KV_HEADS * HEAD_DIM
    group = HEADS // KV_HEADS
    queries = projected[:, :width].reshape(rows, KV_HEADS, group, HEAD_DIM)
    keys = projected[:, width:width + kv_width].reshape(rows, KV_HEADS, HEAD_DIM)
    values = projected[:, width + kv_width:].reshape(rows, KV_HEADS, HEAD_DIM)
    block = min(512, rows)
    count = rows // block
    places = jnp.arange(rows)

    def one_block(piece):
        query_part, seg_part, place_part = piece
        scores = jnp.einsum('tgjd,sgd->tgjs', query_part, keys, precision=HIGH) * HEAD_DIM ** (-0.5)
        scores = low_back(scores)
        allowed = (seg_part[:, None] == segments[None, :]) & (places[None, :] <= place_part[:, None])
        probs = jax.nn.softmax(jnp.where(allowed[:, None, None, :], scores, -1e+30), axis=-1)
        return jnp.einsum('tgjs,sgd->tgjd', probs, values, precision=HIGH)
    blocks_out = lax.map(jax.checkpoint(one_block), (queries.reshape(count, block, KV_HEADS, group, HEAD_DIM), segments.reshape(count, block), places.reshape(count, block)))
    return blocks_out.reshape(rows, width)

def layer(tokens, input_gain, ssm_input, state_proj, step_proj, ssm_output, qkv_proj, attn_output, ffn_gain, gate_up, down_proj, head_params, segments):
    live = jnp.where(segments >= 0, jnp.ones_like(tokens[:, 0]), jnp.zeros_like(tokens[:, 0]))[:, None]
    normed = low(norm_rows(tokens, input_gain))
    inner = rounded(matmul(normed, ssm_input))
    states = rounded(matmul(normed, state_proj))
    step_raw = low_back(matmul(normed, step_proj))
    projected = rounded(matmul(normed, qkv_proj))
    gated = rounded(mamba_group(inner, states, step_raw, head_params, segments))
    attended = rounded(attend_group(projected, segments))
    mixed_out = low_back(matmul(gated, ssm_output.T) + matmul(attended, attn_output.T))
    hidden = tokens + live * mixed_out
    normed2 = low(norm_rows(hidden, ffn_gain))
    gate_vals = low_back(matmul(normed2, gate_up))
    activated = low(jax.nn.silu(gate_vals[:, :FF]) * gate_vals[:, FF:])
    return hidden + live * matmul(activated, down_proj.T)

def reference(tokens, cotangent, segment_ids, input_gain, ssm_input, state_proj, step_proj, ssm_output, qkv_proj, attn_output, ffn_gain, gate_up, down_proj, head_params):
    params = (input_gain.astype(jnp.float32), ssm_input.astype(jnp.float32), state_proj.astype(jnp.float32), step_proj.astype(jnp.float32), ssm_output.astype(jnp.float32), qkv_proj.astype(jnp.float32), attn_output.astype(jnp.float32), ffn_gain.astype(jnp.float32), gate_up.astype(jnp.float32), down_proj.astype(jnp.float32), head_params)

    def per_group(sums, piece):
        group_tokens, group_cot, group_segs = piece

        def forward(inputs, *weights):
            return layer(inputs, *weights, group_segs)
        result, pullback = jax.vjp(forward, group_tokens.astype(jnp.float32), *params)
        grads = pullback(group_cot.astype(jnp.float32))
        sums = tuple((total + extra for total, extra in zip(sums, grads[1:])))
        return (sums, (result.astype(jnp.bfloat16), grads[0].astype(jnp.bfloat16)))
    empty = tuple((jnp.zeros_like(weight) for weight in params))
    sums, outputs = lax.scan(per_group, empty, (tokens, cotangent, segment_ids))
    return (outputs[0], outputs[1], sums[0], sums[1], sums[2], sums[3], sums[4], sums[5], sums[6], sums[7], sums[8], sums[9], sums[10])
```

```python
import math

import jax
import jax.numpy as jnp
from jax import lax
from jax.sharding import PartitionSpec as P

FF = 2048
HEADS = 8
KV_HEADS = 2
HEAD_DIM = 64
SSM_HEADS = 24
SSM_DIM = 64
STATE = 128
D_SSM = 1536


EPS = 1e-06
WIDE = 128
HIGH = lax.Precision.HIGHEST


def project(left, right):
    return jnp.dot(left, right, preferred_element_type=jnp.float32)


def project_back(left, right):
    return lax.dot_general(
        left, right, (((1,), (1,)), ((), ())), preferred_element_type=jnp.float32
    )


def outer_sum(left, right):
    return lax.dot_general(
        left, right, (((0,), (0,)), ((), ())), preferred_element_type=jnp.float32
    )


def norm_rows(values, gain):
    inverse = lax.rsqrt(jnp.mean(values * values, axis=-1, keepdims=True) + EPS)
    return (values * inverse * gain, inverse)


def norm_back(grad, values, inverse, gain):
    scaled = values * inverse
    gain_grad = jnp.sum(grad * scaled, axis=0)
    weighted = grad * gain
    return (
        inverse * (weighted - scaled * jnp.mean(weighted * scaled, axis=-1, keepdims=True)),
        gain_grad,
    )


def heads_first(values, kind=jnp.bfloat16):
    rows = values.shape[0]
    return values.astype(kind).reshape(rows, SSM_HEADS, SSM_DIM).transpose(1, 0, 2)


def rows_first(values):
    return values.transpose(1, 0, 2).reshape(values.shape[1], D_SSM)


def spread_heads(values):
    return jnp.repeat(values, SSM_DIM, axis=-1)


def sum_heads(values):
    return jnp.sum(values.reshape(values.shape[0], SSM_HEADS, SSM_DIM), axis=-1)


def running_sum(values, reverse=False):
    places = jnp.arange(values.shape[0])
    if reverse:
        lower = places[None, :] >= places[:, None]
    else:
        lower = places[None, :] <= places[:, None]
    return jnp.dot(lower.astype(jnp.float32), values, precision=HIGH)


def decay_grid(cumul, masked):
    columns = cumul.T
    spread = columns[:, :, None] - columns[:, None, :]
    return jnp.exp(jnp.minimum(spread, 0.0)) * masked[None]


def link_weights(decays, firsts, lasts, place):
    count = decays.shape[0]
    keeps = jnp.where(firsts[1:] == lasts[:-1], 1.0, 0.0)
    keeps = jnp.concatenate([jnp.zeros_like(keeps[:1]), keeps])
    steps = decays * keeps[:, None]
    index = jnp.arange(count)
    source, middle = index[:, None, None], index[None, :, None]
    ahead = (source < middle) & (middle < place)
    ahead_product = jnp.prod(jnp.where(ahead, steps[None], 1.0), axis=1)
    own_keep = jnp.sum(jnp.where(index == place, keeps, 0.0))
    entry_weight = jnp.where((index < place)[:, None], ahead_product, 0.0) * own_keep
    behind = (place < middle) & (middle < source)
    behind_product = jnp.prod(jnp.where(behind, steps[None], 1.0), axis=1)
    exit_weight = jnp.where((index > place)[:, None], behind_product, 0.0) * keeps[:, None]
    return entry_weight, exit_weight


def weigh_states(weights, gathered):
    states = gathered.astype(jnp.float32).reshape(-1, SSM_HEADS, SSM_DIM, STATE)
    return jnp.sum(weights[:, :, None, None] * states, axis=0).reshape(D_SSM, STATE)


def visible(seg_float, seg_piece, query_pos, start, span):
    key_pos = start + jnp.arange(span)
    same = seg_float[:, None] == seg_piece.astype(jnp.float32)[None, :]
    causal = key_pos[None, :] <= query_pos[:, None]
    return (same & causal)[:, None, None, :]


def body(
    tokens,
    cotangent,
    segment_ids,
    input_gain,
    ssm_input,
    state_proj,
    step_proj,
    ssm_output,
    qkv_proj,
    attn_output,
    ffn_gain,
    gate_up,
    down_proj,
    head_params,
):
    rows = tokens.shape[1]
    width = HEADS * HEAD_DIM
    kv_width = KV_HEADS * HEAD_DIM
    group = HEADS // KV_HEADS
    scale = HEAD_DIM ** (-0.5)
    shard_rows = ssm_input.shape[0]
    padding = jnp.zeros((shard_rows, WIDE - SSM_HEADS - 2), jnp.bfloat16)
    first_full = lax.all_gather(
        jnp.concatenate(
            [
                ssm_input,
                qkv_proj,
                state_proj,
                step_proj,
                input_gain[:, None],
                ffn_gain[:, None],
                padding,
            ],
            axis=1,
        ),
        ("seq", "rep"),
        axis=0,
        tiled=True,
    )
    second_full = lax.all_gather(
        jnp.concatenate([ssm_output, attn_output, gate_up, down_proj], axis=1),
        ("seq", "rep"),
        axis=0,
        tiled=True,
    )
    qkv_at = 2 * D_SSM
    states_at = qkv_at + width + 2 * kv_width
    step_at = states_at + 2 * STATE
    gate_at = D_SSM + width
    down_at = gate_at + 2 * FF
    gain_first = first_full[:, step_at + SSM_HEADS]
    gain_second = first_full[:, step_at + SSM_HEADS + 1]
    out_full = second_full[:, :gate_at]
    gate_full = second_full[:, gate_at:down_at]
    down_full = second_full[:, down_at:]
    resident = tokens[0].astype(jnp.float32)
    segments = segment_ids[0]
    live = jnp.where(segments >= 0, 1.0, 0.0)[:, None]
    first_gain = gain_first.astype(jnp.float32)
    normed_float, inverse_one = norm_rows(resident, first_gain)
    normed = normed_float.astype(jnp.bfloat16)
    entered = project(normed, first_full)
    inner = entered[:, :qkv_at].astype(jnp.bfloat16)
    projected = entered[:, qkv_at:states_at].astype(jnp.bfloat16)
    states = entered[:, states_at:step_at].astype(jnp.bfloat16)
    step_raw = entered[:, step_at : step_at + SSM_HEADS]
    queries = projected[:, :width].reshape(rows, KV_HEADS, group, HEAD_DIM)
    key_vals = projected[:, width:]
    seg_float = segments.astype(jnp.float32)
    kv_wire = jnp.concatenate(
        [
            key_vals,
            segments.astype(jnp.bfloat16)[:, None],
            jnp.zeros((rows, WIDE - 1), jnp.bfloat16),
        ],
        axis=1,
    )
    kv_gathered = lax.all_gather(kv_wire, "seq", axis=0, tiled=True)
    kv_all = kv_gathered[:, : 2 * kv_width]
    seg_all = kv_gathered[:, 2 * kv_width]

    signal_low = inner[:, D_SSM:]
    signal = signal_low.astype(jnp.float32)
    gate_float = inner[:, :D_SSM].astype(jnp.float32)
    entry_map, read_map = states[:, :STATE], states[:, STATE:]
    earlier = jnp.concatenate([segments[:1], segments[:-1]])
    restarts = jnp.where(segments != earlier, 1.0, 0.0)
    shifted = step_raw + head_params[1]
    step_size = jax.nn.softplus(shifted)
    log_decay = -step_size * jnp.exp(head_params[0])
    cumul = running_sum(log_decay)
    counter = running_sum(restarts[:, None])[:, 0]
    places = jnp.arange(rows)
    joined = (counter[:, None] == counter[None, :]) & (places[None, :] <= places[:, None])
    joined = jnp.where(joined, 1.0, 0.0)
    crossing = project_back(read_map, entry_map) * joined
    reach = jnp.where((counter == 0)[:, None], jnp.exp(cumul), 0.0)
    closing = jnp.where((counter == counter[-1])[:, None], jnp.exp(cumul[-1][None, :] - cumul), 0.0)
    closing_step = spread_heads(closing * step_size)
    closed = (signal * closing_step).astype(jnp.bfloat16)
    ending = outer_sum(closed, entry_map)
    decay = reach[-1]
    decay_high = decay.astype(jnp.bfloat16)
    decay_low = (decay - decay_high.astype(jnp.float32)).astype(jnp.bfloat16)
    edges = jnp.stack([segments[0], segments[-1]]).astype(jnp.bfloat16)
    notes = jnp.concatenate(
        [decay_high, decay_low, edges, jnp.zeros((16 * STATE - 2 * SSM_HEADS - 2,), jnp.bfloat16)]
    ).reshape(16, STATE)
    state_wire = jnp.concatenate([ending.astype(jnp.bfloat16), notes], axis=0)
    state_gathered = lax.all_gather(state_wire, "seq", axis=0)
    noted = state_gathered[:, D_SSM].astype(jnp.float32)
    place = lax.axis_index("seq")
    entry_weight, exit_weight = link_weights(
        noted[:, :SSM_HEADS] + noted[:, SSM_HEADS : 2 * SSM_HEADS],
        noted[:, 2 * SSM_HEADS],
        noted[:, 2 * SSM_HEADS + 1],
        place,
    )
    signal_heads = heads_first(signal_low)
    mixing = decay_grid(cumul, crossing) * step_size.T[:, None, :]
    mixing_low = mixing.astype(jnp.bfloat16)
    within = jnp.einsum(
        "hts,hsp->htp", mixing_low, signal_heads, preferred_element_type=jnp.float32
    )
    skip = spread_heads(head_params[2])[None]
    reach_wide = spread_heads(reach)
    mixed_zero = rows_first(within) + skip * signal
    entry = weigh_states(entry_weight, state_gathered[:, :D_SSM])
    entry_low = entry.astype(jnp.bfloat16)
    read_entry = project_back(read_map, entry_low)
    mixed = mixed_zero + reach_wide * read_entry
    sig_gate = jax.nn.sigmoid(gate_float)
    gated = (mixed * gate_float * sig_gate).astype(jnp.bfloat16)
    row_start = lax.axis_index("seq") * rows
    query_pos = row_start + jnp.arange(rows)
    row_last = row_start + rows - 1
    span = kv_all.shape[0]

    keys_all = kv_all[:, :kv_width].reshape(span, KV_HEADS, HEAD_DIM)
    values_all = kv_all[:, kv_width:].reshape(span, KV_HEADS, HEAD_DIM)
    scores_all = (
        jnp.einsum("tgjd,sgd->tgjs", queries, keys_all, preferred_element_type=jnp.float32) * scale
    )
    allowed_all = visible(seg_float, seg_all, query_pos, 0, span)
    masked = jnp.where(allowed_all, scores_all, -1e30)
    top = jnp.max(masked, axis=-1)
    weights_all = jnp.where(allowed_all, jnp.exp(masked - top[..., None]), 0.0)
    total = jnp.sum(weights_all, axis=-1)
    weighted = jnp.einsum(
        "tgjs,sgd->tgjd",
        weights_all.astype(jnp.bfloat16),
        values_all,
        preferred_element_type=jnp.float32,
    )
    attended_float = weighted / total[..., None]
    log_total = top + jnp.log(total)
    attended = attended_float.reshape(rows, width).astype(jnp.bfloat16)
    mixed_low = jnp.concatenate([gated, attended], axis=1)
    mixed_out = project_back(mixed_low, out_full)
    hidden = resident + live * mixed_out
    second_gain = gain_second.astype(jnp.float32)
    normed2_float, inverse_two = norm_rows(hidden, second_gain)
    normed2 = normed2_float.astype(jnp.bfloat16)
    gate_vals = project(normed2, gate_full)
    gate_part = gate_vals[:, :FF]
    up_part = gate_vals[:, FF:]
    sigma = jax.nn.sigmoid(gate_part)
    activated = (gate_part * sigma * up_part).astype(jnp.bfloat16)
    result = hidden + live * project_back(activated, down_full)
    layer_out = result.astype(jnp.bfloat16)[None]
    upstream = cotangent[0].astype(jnp.float32)
    ffn_wire = (live * upstream).astype(jnp.bfloat16)
    down_grad = outer_sum(ffn_wire, activated)
    activated_grad = project(ffn_wire, down_full)
    gate_grad = activated_grad * up_part * sigma * (1.0 + gate_part * (1.0 - sigma))
    up_grad = activated_grad * gate_part * sigma
    gate_up_wire = jnp.concatenate([gate_grad, up_grad], axis=1).astype(jnp.bfloat16)
    gate_up_grad = outer_sum(normed2, gate_up_wire)
    normed2_grad = project_back(gate_up_wire, gate_full)
    hidden_back, gain_two_grad = norm_back(normed2_grad, hidden, inverse_two, second_gain)
    hidden_grad = upstream + hidden_back
    mixed_wire = (live * hidden_grad).astype(jnp.bfloat16)
    out_proj_grad = outer_sum(mixed_wire, mixed_low)
    mixed_low_wire = project(mixed_wire, out_full).astype(jnp.bfloat16)
    gated_wire = mixed_low_wire[:, :D_SSM].astype(jnp.float32)
    attended_wire = mixed_low_wire[:, D_SSM:]
    mixed_grad = gated_wire * gate_float * sig_gate
    gate_float_grad = gated_wire * mixed * sig_gate * (1.0 + gate_float * (1.0 - sig_gate))
    mixed_grad_low = mixed_grad.astype(jnp.bfloat16)
    reached = (mixed_grad * reach_wide).astype(jnp.bfloat16)
    entry_grad = outer_sum(reached, read_map)
    grad_gathered = lax.all_gather(entry_grad.astype(jnp.bfloat16), "seq", axis=0)
    out_grad = attended_wire.reshape(rows, KV_HEADS, group, HEAD_DIM)
    out_grad_float = out_grad.astype(jnp.float32)
    delta = jnp.sum(out_grad_float * attended_float, axis=-1)
    group_rows = kv_all.shape[0]
    block = math.gcd(group_rows, 512)
    count = group_rows // block

    def key_block(query_sum, piece):
        kv_piece, seg_piece, start = piece

        def key_work(unused):
            keys = kv_piece[:, :kv_width].reshape(block, KV_HEADS, HEAD_DIM)
            values = kv_piece[:, kv_width:].reshape(block, KV_HEADS, HEAD_DIM)
            scores = (
                jnp.einsum("tgjd,sgd->tgjs", queries, keys, preferred_element_type=jnp.float32)
                * scale
            )
            allowed = visible(seg_float, seg_piece, query_pos, start, block)
            probability = jnp.where(
                allowed, jnp.exp(jnp.where(allowed, scores - log_total[..., None], -1e30)), 0.0
            )
            values_grad = jnp.einsum(
                "tgjs,tgjd->sgd",
                probability.astype(jnp.bfloat16),
                out_grad,
                preferred_element_type=jnp.float32,
            )
            prob_grad = jnp.einsum(
                "tgjd,sgd->tgjs", out_grad, values, preferred_element_type=jnp.float32
            )
            score_wire = (probability * (prob_grad - delta[..., None])).astype(jnp.bfloat16)
            query_part = (
                jnp.einsum("tgjs,sgd->tgjd", score_wire, keys, preferred_element_type=jnp.float32)
                * scale
            )
            keys_grad = (
                jnp.einsum(
                    "tgjs,tgjd->sgd", score_wire, queries, preferred_element_type=jnp.float32
                )
                * scale
            )
            block_grad = jnp.concatenate(
                [keys_grad.reshape(block, kv_width), values_grad.reshape(block, kv_width)], axis=1
            )
            return (query_part, block_grad)

        def skip(unused):
            return (jnp.zeros_like(query_sum), jnp.zeros((block, 2 * kv_width), jnp.float32))

        query_part, block_grad = lax.cond(start <= row_last, key_work, skip, 0)
        return (query_sum + query_part, block_grad)

    starts = jnp.arange(count) * block
    query_grad, key_grads = lax.scan(
        key_block,
        jnp.zeros((rows, KV_HEADS, group, HEAD_DIM), jnp.float32),
        (kv_all.reshape(count, block, 2 * kv_width), seg_all.reshape(count, block), starts),
    )
    own_kv = lax.psum_scatter(
        key_grads.reshape(group_rows, 2 * kv_width).astype(jnp.bfloat16),
        "seq",
        scatter_dimension=0,
        tiled=True,
    ).astype(jnp.float32)
    early_grads = jnp.concatenate(
        [
            out_proj_grad.astype(jnp.bfloat16),
            gate_up_grad.astype(jnp.bfloat16),
            down_grad.astype(jnp.bfloat16),
        ],
        axis=1,
    )
    early_grads, own_kv, grad_gathered = lax.optimization_barrier(
        (early_grads, own_kv, grad_gathered)
    )
    early_owned = lax.psum_scatter(
        early_grads, ("seq", "rep"), scatter_dimension=0, tiled=True
    ).astype(jnp.float32)

    end_grad = weigh_states(exit_weight, grad_gathered)
    end_low = end_grad.astype(jnp.bfloat16)
    decay_grad = jnp.sum((end_grad * entry).reshape(SSM_HEADS, -1), axis=1)
    grad_heads = heads_first(mixed_grad_low)
    mixing_grad = jnp.einsum(
        "htp,hsp->hts", grad_heads, signal_heads, preferred_element_type=jnp.float32
    )
    signal_within = jnp.einsum(
        "hts,htp->hsp", mixing_low, grad_heads, preferred_element_type=jnp.float32
    )
    decay_part = decay_grid(cumul, joined)
    crossing_grad = jnp.sum(mixing_grad * decay_part * step_size.T[:, None, :], axis=0).astype(
        jnp.bfloat16
    )
    stepless = mixing_grad * decay_part * crossing[None]
    step_within = jnp.sum(stepless, axis=1).T
    row_within = jnp.sum(stepless * step_size.T[:, None, :], axis=2).T
    end_read = project_back(entry_map, end_low)
    signal_grad = rows_first(signal_within) + end_read * closing_step + skip * mixed_grad
    entry_map_grad = outer_sum(crossing_grad, read_map) + project(closed, end_low)
    read_map_grad = project(crossing_grad, entry_map) + project(reached, entry_low)
    reach_grad = sum_heads(mixed_grad * read_entry)
    closed_grad = sum_heads(end_read * signal)
    closing_part = closed_grad * step_size * closing
    cumul_grad = row_within - step_within * step_size + reach_grad * reach - closing_part
    last_grad = jnp.sum(closing_part, axis=0) + decay_grad * decay
    cumul_grad = cumul_grad + jnp.where((places == rows - 1)[:, None], last_grad[None], 0.0)
    log_grad = running_sum(cumul_grad, reverse=True)
    step_size_grad = step_within + closed_grad * closing - log_grad * jnp.exp(head_params[0])
    step_grad = step_size_grad * jax.nn.sigmoid(shifted)
    head_grad = jnp.stack(
        [
            jnp.sum(log_grad * log_decay, axis=0),
            jnp.sum(step_grad, axis=0),
            jnp.sum(sum_heads(mixed_grad * signal), axis=0),
        ]
    )
    first_wire = jnp.concatenate(
        [
            gate_float_grad.astype(jnp.bfloat16),
            signal_grad.astype(jnp.bfloat16),
            query_grad.reshape(rows, width).astype(jnp.bfloat16),
            own_kv.astype(jnp.bfloat16),
            entry_map_grad.astype(jnp.bfloat16),
            read_map_grad.astype(jnp.bfloat16),
            step_grad.astype(jnp.bfloat16),
            jnp.zeros((rows, WIDE - SSM_HEADS), jnp.bfloat16),
        ],
        axis=1,
    )
    late_owned = lax.psum_scatter(
        outer_sum(normed, first_wire).astype(jnp.bfloat16),
        ("seq", "rep"),
        scatter_dimension=0,
        tiled=True,
    ).astype(jnp.float32)
    normed_grad = project_back(first_wire, first_full)
    resident_back, gain_one_grad = norm_back(normed_grad, resident, inverse_one, first_gain)
    input_grad = (hidden_grad + resident_back).astype(jnp.bfloat16)[None]
    model = resident.shape[1]
    small_sum = lax.psum(
        jnp.concatenate([gain_one_grad, gain_two_grad, head_grad.reshape(-1)]), ("seq", "rep")
    )
    mine = (place * lax.axis_size("rep") + lax.axis_index("rep")) * shard_rows
    return (
        layer_out,
        input_grad,
        lax.dynamic_slice_in_dim(small_sum, mine, shard_rows),
        late_owned[:, :qkv_at],
        late_owned[:, states_at:step_at],
        late_owned[:, step_at : step_at + SSM_HEADS],
        early_owned[:, :D_SSM],
        late_owned[:, qkv_at:states_at],
        early_owned[:, D_SSM:gate_at],
        lax.dynamic_slice_in_dim(small_sum, model + mine, shard_rows),
        early_owned[:, gate_at:down_at],
        early_owned[:, down_at:],
        small_sum[2 * model :].reshape(head_grad.shape),
    )


def solution(mesh):
    placed = (
        P("rep", "seq", None),
        P("rep", "seq", None),
        P("rep", "seq"),
        P(("seq", "rep")),
        P(("seq", "rep"), None),
        P(("seq", "rep"), None),
        P(("seq", "rep"), None),
        P(("seq", "rep"), None),
        P(("seq", "rep"), None),
        P(("seq", "rep"), None),
        P(("seq", "rep")),
        P(("seq", "rep"), None),
        P(("seq", "rep"), None),
        P(),
    )
    return jax.shard_map(
        body,
        mesh=mesh,
        in_specs=placed,
        out_specs=(
            P("rep", "seq", None),
            P("rep", "seq", None),
            P(("seq", "rep")),
            P(("seq", "rep"), None),
            P(("seq", "rep"), None),
            P(("seq", "rep"), None),
            P(("seq", "rep"), None),
            P(("seq", "rep"), None),
            P(("seq", "rep"), None),
            P(("seq", "rep")),
            P(("seq", "rep"), None),
            P(("seq", "rep"), None),
            P(),
        ),
        check_vma=False,
    )
```

```python
import math

import jax
import jax.numpy as jnp
from jax import lax
from jax.sharding import PartitionSpec as P

FF = 2048
HEADS = 8
KV_HEADS = 2
HEAD_DIM = 64
SSM_HEADS = 24
SSM_DIM = 64
STATE = 128
D_SSM = 1536


EPS = 1e-06
WIDE = 128
HIGH = lax.Precision.HIGHEST


def project(left, right):
    return jnp.dot(left, right, preferred_element_type=jnp.float32)


def project_back(left, right):
    return lax.dot_general(
        left, right, (((1,), (1,)), ((), ())), preferred_element_type=jnp.float32
    )


def outer_sum(left, right):
    return lax.dot_general(
        left, right, (((0,), (0,)), ((), ())), preferred_element_type=jnp.float32
    )


def norm_rows(values, gain):
    inverse = lax.rsqrt(jnp.mean(values * values, axis=-1, keepdims=True) + EPS)
    return (values * inverse * gain, inverse)


def norm_back(grad, values, inverse, gain):
    scaled = values * inverse
    gain_grad = jnp.sum(grad * scaled, axis=0)
    weighted = grad * gain
    return (
        inverse * (weighted - scaled * jnp.mean(weighted * scaled, axis=-1, keepdims=True)),
        gain_grad,
    )


def heads_first(values, kind=jnp.bfloat16):
    rows = values.shape[0]
    return values.astype(kind).reshape(rows, SSM_HEADS, SSM_DIM).transpose(1, 0, 2)


def rows_first(values):
    return values.transpose(1, 0, 2).reshape(values.shape[1], D_SSM)


def spread_heads(values):
    return jnp.repeat(values, SSM_DIM, axis=-1)


def sum_heads(values):
    return jnp.sum(values.reshape(values.shape[0], SSM_HEADS, SSM_DIM), axis=-1)


def running_sum(values, reverse=False):
    places = jnp.arange(values.shape[0])
    if reverse:
        lower = places[None, :] >= places[:, None]
    else:
        lower = places[None, :] <= places[:, None]
    return jnp.dot(lower.astype(jnp.float32), values, precision=HIGH)


def decay_grid(cumul, masked):
    columns = cumul.T
    spread = columns[:, :, None] - columns[:, None, :]
    return jnp.exp(jnp.minimum(spread, 0.0)) * masked[None]


def swap(values, bit):
    count = lax.axis_size("seq")
    return lax.ppermute(values, "seq", [(i, i ^ bit) for i in range(count)])


def bits_of(count):
    return [1 << at for at in range(count.bit_length() - 1)]


def gather_blocks(block, place):
    blocks = block[None]
    for bit in reversed(bits_of(lax.axis_size("seq"))):
        arrived = swap(blocks, bit)
        late = (place & bit) != 0
        pair = jnp.stack(
            [jnp.where(late, arrived, blocks), jnp.where(late, blocks, arrived)], axis=1
        )
        blocks = pair.reshape(-1, *block.shape)
    return blocks


def scatter_blocks(blocks, place):
    for bit in bits_of(lax.axis_size("seq")):
        pair = blocks.reshape(-1, 2, *blocks.shape[1:])
        late = (place & bit) != 0
        own = jnp.where(late, pair[:, 1], pair[:, 0])
        other = jnp.where(late, pair[:, 0], pair[:, 1])
        blocks = own + swap(other.astype(jnp.bfloat16), bit).astype(jnp.float32)
    return blocks[0]


def link_steps(decays, firsts, lasts):
    keeps = jnp.where(firsts[1:] == lasts[:-1], 1.0, 0.0)
    keeps = jnp.concatenate([jnp.zeros_like(keeps[:1]), keeps])
    return keeps, decays * keeps[:, None]


def span_product(steps, start, stop):
    index = jnp.arange(steps.shape[0])[:, None]
    inside = (index >= start) & (index < stop)
    return jnp.repeat(jnp.prod(jnp.where(inside, steps, 1.0), axis=0), SSM_DIM)[:, None]


def link_scan(value, steps, place, reverse):
    total, entering = value, jnp.zeros_like(value)
    for bit in bits_of(lax.axis_size("seq")):
        arrived = swap(total.astype(jnp.bfloat16), bit).astype(jnp.float32)
        base = place - place % bit
        far = ((place & bit) == 0) if reverse else ((place & bit) != 0)
        own_span = span_product(steps, base, base + bit)
        other = base ^ bit
        other_span = span_product(steps, other, other + bit)
        if reverse:
            reaching = span_product(steps, place + 1, base + bit)
        else:
            reaching = span_product(steps, base, place)
        entering = entering + jnp.where(far, reaching, 0.0) * arrived
        total = jnp.where(far, total + own_span * arrived, arrived + other_span * total)
    return entering


def visible(seg_float, seg_piece, query_pos, start, span):
    key_pos = start + jnp.arange(span)
    same = seg_float[:, None] == seg_piece.astype(jnp.float32)[None, :]
    causal = key_pos[None, :] <= query_pos[:, None]
    return (same & causal)[:, None, None, :]


def body(
    tokens,
    cotangent,
    segment_ids,
    input_gain,
    ssm_input,
    state_proj,
    step_proj,
    ssm_output,
    qkv_proj,
    attn_output,
    ffn_gain,
    gate_up,
    down_proj,
    head_params,
):
    rows = tokens.shape[1]
    width = HEADS * HEAD_DIM
    kv_width = KV_HEADS * HEAD_DIM
    group = HEADS // KV_HEADS
    scale = HEAD_DIM ** (-0.5)
    shard_rows = ssm_input.shape[0]
    padding = jnp.zeros((shard_rows, WIDE - SSM_HEADS - 2), jnp.bfloat16)
    first_full = lax.all_gather(
        jnp.concatenate(
            [
                ssm_input,
                qkv_proj,
                state_proj,
                step_proj,
                input_gain[:, None],
                ffn_gain[:, None],
                padding,
            ],
            axis=1,
        ),
        ("seq", "rep"),
        axis=0,
        tiled=True,
    )
    second_shard, first_full = lax.optimization_barrier(
        (jnp.concatenate([ssm_output, attn_output, gate_up, down_proj], axis=1), first_full)
    )
    second_full = lax.all_gather(second_shard, ("seq", "rep"), axis=0, tiled=True)
    qkv_at = 2 * D_SSM
    states_at = qkv_at + width + 2 * kv_width
    step_at = states_at + 2 * STATE
    gate_at = D_SSM + width
    down_at = gate_at + 2 * FF
    gain_first = first_full[:, step_at + SSM_HEADS]
    gain_second = first_full[:, step_at + SSM_HEADS + 1]
    out_full = second_full[:, :gate_at]
    gate_full = second_full[:, gate_at:down_at]
    down_full = second_full[:, down_at:]
    resident = tokens[0].astype(jnp.float32)
    segments = segment_ids[0]
    live = jnp.where(segments >= 0, 1.0, 0.0)[:, None]
    first_gain = gain_first.astype(jnp.float32)
    normed_float, inverse_one = norm_rows(resident, first_gain)
    normed = normed_float.astype(jnp.bfloat16)
    entered = project(normed, first_full)
    inner = entered[:, :qkv_at].astype(jnp.bfloat16)
    projected = entered[:, qkv_at:states_at].astype(jnp.bfloat16)
    states = entered[:, states_at:step_at].astype(jnp.bfloat16)
    step_raw = entered[:, step_at : step_at + SSM_HEADS]
    queries = projected[:, :width].reshape(rows, KV_HEADS, group, HEAD_DIM)
    key_vals = projected[:, width:]
    seg_float = segments.astype(jnp.float32)
    signal_low = inner[:, D_SSM:]
    signal = signal_low.astype(jnp.float32)
    gate_float = inner[:, :D_SSM].astype(jnp.float32)
    entry_map, read_map = states[:, :STATE], states[:, STATE:]
    earlier = jnp.concatenate([segments[:1], segments[:-1]])
    restarts = jnp.where(segments != earlier, 1.0, 0.0)
    shifted = step_raw + head_params[1]
    step_size = jax.nn.softplus(shifted)
    log_decay = -step_size * jnp.exp(head_params[0])
    cumul = running_sum(log_decay)
    counter = running_sum(restarts[:, None])[:, 0]
    places = jnp.arange(rows)
    joined = (counter[:, None] == counter[None, :]) & (places[None, :] <= places[:, None])
    joined = jnp.where(joined, 1.0, 0.0)
    crossing = project_back(read_map, entry_map) * joined
    reach = jnp.where((counter == 0)[:, None], jnp.exp(cumul), 0.0)
    decay = reach[-1]
    decay_high = decay.astype(jnp.bfloat16)
    decay_low = (decay - decay_high.astype(jnp.float32)).astype(jnp.bfloat16)
    note_size = 2 * SSM_HEADS + rows
    note_rows = 16 * (-(-note_size // (16 * 2 * kv_width)))
    notes = jnp.concatenate(
        [
            decay_high,
            decay_low,
            segments.astype(jnp.bfloat16),
            jnp.zeros((note_rows * 2 * kv_width - note_size,), jnp.bfloat16),
        ]
    ).reshape(note_rows, 2 * kv_width)
    place = lax.axis_index("seq")
    kv_blocks = gather_blocks(jnp.concatenate([key_vals, notes], axis=0), place)
    group_rows = kv_blocks.shape[0] * rows
    kv_all = kv_blocks[:, :rows].reshape(group_rows, 2 * kv_width)
    noted = kv_blocks[:, rows:].reshape(kv_blocks.shape[0], -1)
    seg_blocks = noted[:, 2 * SSM_HEADS : note_size].astype(jnp.float32)
    seg_all = seg_blocks.reshape(group_rows)
    decays = noted[:, : 2 * SSM_HEADS].astype(jnp.float32)
    keeps, steps = link_steps(
        decays[:, :SSM_HEADS] + decays[:, SSM_HEADS:], seg_blocks[:, 0], seg_blocks[:, -1]
    )
    own_keep = jnp.sum(jnp.where(jnp.arange(keeps.shape[0]) == place, keeps, 0.0))
    closing = jnp.where((counter == counter[-1])[:, None], jnp.exp(cumul[-1][None, :] - cumul), 0.0)
    closing_step = spread_heads(closing * step_size)
    closed = (signal * closing_step).astype(jnp.bfloat16)
    ending = outer_sum(closed, entry_map)
    signal_heads = heads_first(signal_low)
    mixing = decay_grid(cumul, crossing) * step_size.T[:, None, :]
    mixing_low = mixing.astype(jnp.bfloat16)
    within = jnp.einsum(
        "hts,hsp->htp", mixing_low, signal_heads, preferred_element_type=jnp.float32
    )
    skip = spread_heads(head_params[2])[None]
    reach_wide = spread_heads(reach)
    mixed_zero = rows_first(within) + skip * signal
    entry = own_keep * link_scan(ending, steps, place, False)
    entry_low = entry.astype(jnp.bfloat16)
    read_entry = project_back(read_map, entry_low)
    mixed = mixed_zero + reach_wide * read_entry
    sig_gate = jax.nn.sigmoid(gate_float)
    gated = (mixed * gate_float * sig_gate).astype(jnp.bfloat16)
    row_start = lax.axis_index("seq") * rows
    query_pos = row_start + jnp.arange(rows)
    row_last = row_start + rows - 1
    span = kv_all.shape[0]

    keys_all = kv_all[:, :kv_width].reshape(span, KV_HEADS, HEAD_DIM)
    values_all = kv_all[:, kv_width:].reshape(span, KV_HEADS, HEAD_DIM)
    scores_all = (
        jnp.einsum("tgjd,sgd->tgjs", queries, keys_all, preferred_element_type=jnp.float32) * scale
    )
    allowed_all = visible(seg_float, seg_all, query_pos, 0, span)
    masked = jnp.where(allowed_all, scores_all, -1e30)
    top = jnp.max(masked, axis=-1)
    weights_all = jnp.where(allowed_all, jnp.exp(masked - top[..., None]), 0.0)
    total = jnp.sum(weights_all, axis=-1)
    weighted = jnp.einsum(
        "tgjs,sgd->tgjd",
        weights_all.astype(jnp.bfloat16),
        values_all,
        preferred_element_type=jnp.float32,
    )
    attended_float = weighted / total[..., None]
    log_total = top + jnp.log(total)
    attended = attended_float.reshape(rows, width).astype(jnp.bfloat16)
    mixed_low = jnp.concatenate([gated, attended], axis=1)
    mixed_out = project_back(mixed_low, out_full)
    hidden = resident + live * mixed_out
    second_gain = gain_second.astype(jnp.float32)
    normed2_float, inverse_two = norm_rows(hidden, second_gain)
    normed2 = normed2_float.astype(jnp.bfloat16)
    gate_vals = project(normed2, gate_full)
    gate_part = gate_vals[:, :FF]
    up_part = gate_vals[:, FF:]
    sigma = jax.nn.sigmoid(gate_part)
    activated = (gate_part * sigma * up_part).astype(jnp.bfloat16)
    result = hidden + live * project_back(activated, down_full)
    layer_out = result.astype(jnp.bfloat16)[None]
    upstream = cotangent[0].astype(jnp.float32)
    ffn_wire = (live * upstream).astype(jnp.bfloat16)
    down_grad = outer_sum(ffn_wire, activated)
    activated_grad = project(ffn_wire, down_full)
    gate_grad = activated_grad * up_part * sigma * (1.0 + gate_part * (1.0 - sigma))
    up_grad = activated_grad * gate_part * sigma
    gate_up_wire = jnp.concatenate([gate_grad, up_grad], axis=1).astype(jnp.bfloat16)
    gate_up_grad = outer_sum(normed2, gate_up_wire)
    normed2_grad = project_back(gate_up_wire, gate_full)
    hidden_back, gain_two_grad = norm_back(normed2_grad, hidden, inverse_two, second_gain)
    hidden_grad = upstream + hidden_back
    mixed_wire = (live * hidden_grad).astype(jnp.bfloat16)
    out_proj_grad = outer_sum(mixed_wire, mixed_low)
    mixed_low_wire = project(mixed_wire, out_full).astype(jnp.bfloat16)
    gated_wire = mixed_low_wire[:, :D_SSM].astype(jnp.float32)
    attended_wire = mixed_low_wire[:, D_SSM:]
    mixed_grad = gated_wire * gate_float * sig_gate
    gate_float_grad = gated_wire * mixed * sig_gate * (1.0 + gate_float * (1.0 - sig_gate))
    mixed_grad_low = mixed_grad.astype(jnp.bfloat16)
    reached = (mixed_grad * reach_wide).astype(jnp.bfloat16)
    entry_grad = outer_sum(reached, read_map)
    end_grad = link_scan(own_keep * entry_grad, steps, place, True)
    out_grad = attended_wire.reshape(rows, KV_HEADS, group, HEAD_DIM)
    out_grad_float = out_grad.astype(jnp.float32)
    delta = jnp.sum(out_grad_float * attended_float, axis=-1)
    block = math.gcd(group_rows, 512)
    count = group_rows // block

    def key_block(query_sum, piece):
        kv_piece, seg_piece, start = piece

        def key_work(unused):
            keys = kv_piece[:, :kv_width].reshape(block, KV_HEADS, HEAD_DIM)
            values = kv_piece[:, kv_width:].reshape(block, KV_HEADS, HEAD_DIM)
            scores = (
                jnp.einsum("tgjd,sgd->tgjs", queries, keys, preferred_element_type=jnp.float32)
                * scale
            )
            allowed = visible(seg_float, seg_piece, query_pos, start, block)
            probability = jnp.where(
                allowed, jnp.exp(jnp.where(allowed, scores - log_total[..., None], -1e30)), 0.0
            )
            values_grad = jnp.einsum(
                "tgjs,tgjd->sgd",
                probability.astype(jnp.bfloat16),
                out_grad,
                preferred_element_type=jnp.float32,
            )
            prob_grad = jnp.einsum(
                "tgjd,sgd->tgjs", out_grad, values, preferred_element_type=jnp.float32
            )
            score_wire = (probability * (prob_grad - delta[..., None])).astype(jnp.bfloat16)
            query_part = (
                jnp.einsum("tgjs,sgd->tgjd", score_wire, keys, preferred_element_type=jnp.float32)
                * scale
            )
            keys_grad = (
                jnp.einsum(
                    "tgjs,tgjd->sgd", score_wire, queries, preferred_element_type=jnp.float32
                )
                * scale
            )
            block_grad = jnp.concatenate(
                [keys_grad.reshape(block, kv_width), values_grad.reshape(block, kv_width)], axis=1
            )
            return (query_part, block_grad)

        def skip(unused):
            return (jnp.zeros_like(query_sum), jnp.zeros((block, 2 * kv_width), jnp.float32))

        query_part, block_grad = lax.cond(start <= row_last, key_work, skip, 0)
        return (query_sum + query_part, block_grad)

    starts = jnp.arange(count) * block
    query_grad, key_grads = lax.scan(
        key_block,
        jnp.zeros((rows, KV_HEADS, group, HEAD_DIM), jnp.float32),
        (kv_all.reshape(count, block, 2 * kv_width), seg_all.reshape(count, block), starts),
    )
    own_kv = scatter_blocks(key_grads.reshape(-1, rows, 2 * kv_width), place)
    early_grads = jnp.concatenate(
        [
            out_proj_grad.astype(jnp.bfloat16),
            gate_up_grad.astype(jnp.bfloat16),
            down_grad.astype(jnp.bfloat16),
        ],
        axis=1,
    )
    early_owned = lax.psum_scatter(
        early_grads, ("seq", "rep"), scatter_dimension=0, tiled=True
    )

    end_low = end_grad.astype(jnp.bfloat16)
    decay_grad = jnp.sum((end_grad * entry).reshape(SSM_HEADS, -1), axis=1)
    grad_heads = heads_first(mixed_grad_low)
    mixing_grad = jnp.einsum(
        "htp,hsp->hts", grad_heads, signal_heads, preferred_element_type=jnp.float32
    )
    signal_within = jnp.einsum(
        "hts,htp->hsp", mixing_low, grad_heads, preferred_element_type=jnp.float32
    )
    decay_part = decay_grid(cumul, joined)
    crossing_grad = jnp.sum(mixing_grad * decay_part * step_size.T[:, None, :], axis=0).astype(
        jnp.bfloat16
    )
    stepless = mixing_grad * decay_part * crossing[None]
    step_within = jnp.sum(stepless, axis=1).T
    row_within = jnp.sum(stepless * step_size.T[:, None, :], axis=2).T
    end_read = project_back(entry_map, end_low)
    signal_grad = rows_first(signal_within) + end_read * closing_step + skip * mixed_grad
    entry_map_grad = outer_sum(crossing_grad, read_map) + project(closed, end_low)
    read_map_grad = project(crossing_grad, entry_map) + project(reached, entry_low)
    reach_grad = sum_heads(mixed_grad * read_entry)
    closed_grad = sum_heads(end_read * signal)
    closing_part = closed_grad * step_size * closing
    cumul_grad = row_within - step_within * step_size + reach_grad * reach - closing_part
    last_grad = jnp.sum(closing_part, axis=0) + decay_grad * decay
    cumul_grad = cumul_grad + jnp.where((places == rows - 1)[:, None], last_grad[None], 0.0)
    log_grad = running_sum(cumul_grad, reverse=True)
    step_size_grad = step_within + closed_grad * closing - log_grad * jnp.exp(head_params[0])
    step_grad = step_size_grad * jax.nn.sigmoid(shifted)
    head_grad = jnp.stack(
        [
            jnp.sum(log_grad * log_decay, axis=0),
            jnp.sum(step_grad, axis=0),
            jnp.sum(sum_heads(mixed_grad * signal), axis=0),
        ]
    )
    first_wire = jnp.concatenate(
        [
            gate_float_grad.astype(jnp.bfloat16),
            signal_grad.astype(jnp.bfloat16),
            query_grad.reshape(rows, width).astype(jnp.bfloat16),
            own_kv.astype(jnp.bfloat16),
            entry_map_grad.astype(jnp.bfloat16),
            read_map_grad.astype(jnp.bfloat16),
            step_grad.astype(jnp.bfloat16),
            jnp.zeros((rows, WIDE - SSM_HEADS), jnp.bfloat16),
        ],
        axis=1,
    )
    late_grads, early_owned = lax.optimization_barrier(
        (outer_sum(normed, first_wire).astype(jnp.bfloat16), early_owned)
    )
    late_owned = lax.psum_scatter(
        late_grads, ("seq", "rep"), scatter_dimension=0, tiled=True
    ).astype(jnp.float32)
    early_owned = early_owned.astype(jnp.float32)
    normed_grad = project_back(first_wire, first_full)
    resident_back, gain_one_grad = norm_back(normed_grad, resident, inverse_one, first_gain)
    input_grad = (hidden_grad + resident_back).astype(jnp.bfloat16)[None]
    model = resident.shape[1]
    small_sum = lax.psum(
        jnp.concatenate([gain_one_grad, gain_two_grad, head_grad.reshape(-1)]), ("seq", "rep")
    )
    mine = (place * lax.axis_size("rep") + lax.axis_index("rep")) * shard_rows
    return (
        layer_out,
        input_grad,
        lax.dynamic_slice_in_dim(small_sum, mine, shard_rows),
        late_owned[:, :qkv_at],
        late_owned[:, states_at:step_at],
        late_owned[:, step_at : step_at + SSM_HEADS],
        early_owned[:, :D_SSM],
        late_owned[:, qkv_at:states_at],
        early_owned[:, D_SSM:gate_at],
        lax.dynamic_slice_in_dim(small_sum, model + mine, shard_rows),
        early_owned[:, gate_at:down_at],
        early_owned[:, down_at:],
        small_sum[2 * model :].reshape(head_grad.shape),
    )


def solution(mesh):
    placed = (
        P("rep", "seq", None),
        P("rep", "seq", None),
        P("rep", "seq"),
        P(("seq", "rep")),
        P(("seq", "rep"), None),
        P(("seq", "rep"), None),
        P(("seq", "rep"), None),
        P(("seq", "rep"), None),
        P(("seq", "rep"), None),
        P(("seq", "rep"), None),
        P(("seq", "rep")),
        P(("seq", "rep"), None),
        P(("seq", "rep"), None),
        P(),
    )
    return jax.shard_map(
        body,
        mesh=mesh,
        in_specs=placed,
        out_specs=(
            P("rep", "seq", None),
            P("rep", "seq", None),
            P(("seq", "rep")),
            P(("seq", "rep"), None),
            P(("seq", "rep"), None),
            P(("seq", "rep"), None),
            P(("seq", "rep"), None),
            P(("seq", "rep"), None),
            P(("seq", "rep"), None),
            P(("seq", "rep")),
            P(("seq", "rep"), None),
            P(("seq", "rep"), None),
            P(),
        ),
        check_vma=False,
    )
```
